32 devices in a mesh: dp: 8 (over y, x, core), fsdp: 4 (over z).
Axes of the slice: x: 2, y: 2, z: 4, core: 2. Of those that a mesh axis runs over, the one named last changes fastest.
Arguments:
- unit_ids: int32 [4, 8, 8, 32], P('fsdp', 'dp'), may hold values from 0 to 2047
- session_ids: int32 [4, 8, 8, 32], P('fsdp', 'dp'), may hold values from 0 to 63
- counts: int32 [4, 8, 8], P('fsdp', 'dp'), may hold values from 8 to 32, as said below
- targets: int32 [4, 8, 256, 512], P('fsdp', 'dp'), may hold values 0 or 1
- unit_table: bfloat16 [2048, 1024], replicated, may hold values from -6 to 6
- session_table: bfloat16 [64, 1024], replicated, may hold values from -4 to 4
- attn_weights: bfloat16 [4, 1024, 1024], P(None, 'fsdp'), may hold values from -0.1875 to 0.1875
- read_weight: bfloat16 [1024, 512], P('fsdp'), may hold values from -0.1875 to 0.1875
- latents: bfloat16 [256, 1024], P('fsdp')
Outputs:
- event_grad: bfloat16 [4, 8, 8, 32, 1024], P('fsdp', 'dp')
- grad_attn: float32 [4, 1024, 1024], P(None, 'fsdp')
- grad_read: float32 [1024, 512], P('fsdp')
- grad_latents: float32 [256, 1024], P('fsdp')
The draws below stay inside these ranges and needn't reach their ends.
Inputs may be any that keep to these rules, and one draw needn't show every extreme that they name: counts[f, s, d] is how many of the slots from source s to window d are live (the first ones); in every row (f, s) some window receives exactly 32.
All inputs are finite; a program needn't handle non-finite values. No bound on the sum of `targets` on one device may be relied on, other than what follows from the above.
Results may differ from the reference program's by a relative error of at most 0.012.
The reference program's roundings to bfloat16 on the way count: a program that leaves them out, or rounds other values in their place, can miss the bound.
Values may be sent and summed in bfloat16 or wider, within the bound.
A program may use at most 192 MiB of HBM per device.

```python
import math
import jax
import jax.numpy as jnp
import numpy as np
from jax import lax

D = 1024
HEADS = 16
LAT = 256
OUT = 512
UNITS = 2048
SESS = 64
CAP = 32
N_DP = 8
N_FSDP = 4


def draw_counts(key, part):
    first = jax.random.fold_in(key, 11)
    second = jax.random.fold_in(key, 12)
    third = jax.random.fold_in(key, 13)
    fourth = jax.random.fold_in(key, 14)
    full_shape = (N_FSDP, N_DP, N_DP)
    popular = jax.random.randint(first, (N_FSDP, 1, N_DP), 0, 4) == 0
    heavy = jax.random.randint(second, full_shape, CAP // 2, CAP + 1)
    light = jax.random.randint(third, full_shape, CAP // 4, CAP // 2 + 1)
    chosen = jnp.where(popular, heavy, light)
    picked = jax.random.randint(fourth, (N_FSDP, N_DP, 1), 0, N_DP)
    filled = jnp.arange(N_DP, dtype=jnp.int32)[None, None, :] == picked
    return jnp.where(filled, CAP, chosen).astype(jnp.int32)


def draw_latents(key, part):
    values = jax.random.normal(jax.random.fold_in(key, 21), (LAT, D), jnp.float32)
    return values.astype(jnp.bfloat16)


def place_ends(values, rng, smallest, top_value):
    place = [jax.random.randint(jax.random.fold_in(rng, axis), (), 0, length) for axis, length in enumerate(values.shape)]
    widest = values.shape.index(max(values.shape))
    next_to = place[:widest] + [(place[widest] + 1) % values.shape[widest]] + place[widest + 1:]
    return values.at[tuple(place)].set(smallest).at[tuple(next_to)].set(top_value)


def level_of(rng, extent, cuts, low, high):
    gain, own = 1.0, jax.random.fold_in(rng, 6)
    for dim, parts in cuts:
        steps = jnp.exp(jax.random.uniform(jax.random.fold_in(own, dim), (parts,), jnp.float32, low / len(cuts), high / len(cuts)))
        gain = gain * jnp.repeat(steps, extent[dim] // parts).reshape([-1 if axis == dim else 1 for axis in range(len(extent))])
    return gain


def cumulative_ranks(count, lean):
    portions = [(1 << 20) // math.isqrt(standing ** lean) + 1 for standing in range(1, count + 1)]
    scale = 1 + sum(portions) // (1 << 30)
    return np.cumsum(np.array([max(1, weight // scale) for weight in portions]))


def ranked_ids(own_key, extent, amount, lean):
    table = cumulative_ranks(amount, lean)
    ticket = jax.random.randint(jax.random.fold_in(own_key, 1), extent, 0, int(table[amount - 1]))
    standing = jnp.searchsorted(jnp.asarray(table, jnp.int32), ticket, side="right")
    return jax.random.permutation(jax.random.fold_in(own_key, 2), amount)[standing].astype(jnp.int32)


def centred(key, dims, width, most, cuts=(), kind=jnp.bfloat16):
    drawn = jax.random.normal(key, dims, jnp.float32) * width
    if len(cuts) > 0:
        drawn = level_of(key, dims, cuts, -0.22, 0.18) * drawn
    return jnp.clip(drawn, min=-most, max=most).astype(kind)


def setup_inputs(seed: int = 0) -> dict:
    seeds = jax.random.split(jax.random.key(seed), 10)
    return {
        "unit_ids": place_ends(ranked_ids(seeds[0], (N_FSDP, N_DP, N_DP, CAP), UNITS, 1), jax.random.fold_in(seeds[0], 3), 0, UNITS - 1).astype(jnp.int32),
        "session_ids": place_ends(jax.random.randint(seeds[1], (N_FSDP, N_DP, N_DP, CAP), 0, SESS), jax.random.fold_in(seeds[1], 1), 0, SESS - 1).astype(jnp.int32),
        "counts": draw_counts(jax.random.fold_in(seeds[9], 71), 0),
        "targets": place_ends((jax.random.randint(seeds[3], (N_FSDP, N_DP, LAT, OUT), 0, 4) < 1).astype(jnp.int32), jax.random.fold_in(seeds[3], 1), 0, 1),
        "unit_table": centred(seeds[4], (UNITS, D), 1.0, 6.0),
        "session_table": centred(seeds[5], (SESS, D), 0.5, 4.0),
        "attn_weights": centred(seeds[6], (4, D, D), D ** -0.5, 0.1875, ((1, 4),)),
        "read_weight": centred(seeds[7], (D, OUT), D ** -0.5, 0.1875, ((0, 4),)),
        "latents": draw_latents(jax.random.fold_in(seeds[9], 71), 0),
    }


eps = 1e-05

def rms_scale(rows):
    return lax.rsqrt(lax.optimization_barrier(jnp.mean(rows * rows, axis=-1, keepdims=True)) + eps)

def rms_back(rows, factor, grad_out):
    cubed = factor * factor * factor
    return factor * grad_out - rows * cubed * lax.optimization_barrier(jnp.mean(grad_out * rows, axis=-1, keepdims=True))

def matmul(left, right):
    return jnp.dot(left, right, preferred_element_type=jnp.float32)

def contract(form, left, right):
    return jnp.einsum(form, left.astype(jnp.float32), right.astype(jnp.float32))

def event_front(tokens, w_key, w_value):
    token_rows = tokens.astype(jnp.float32)
    factor = rms_scale(token_rows)
    normed = (token_rows * factor).astype(jnp.bfloat16)
    key_rows = matmul(normed, w_key).astype(jnp.bfloat16)
    value_rows = matmul(normed, w_value).astype(jnp.bfloat16)
    return (normed, factor, key_rows, value_rows)

def event_back(tokens, factor, normed, grad_keys, grad_values, w_key, w_value):
    grad_wkey = matmul(normed.T, grad_keys)
    grad_wvalue = matmul(normed.T, grad_values)
    grad_normed = matmul(grad_keys, w_key.T) + matmul(grad_values, w_value.T)
    grad_tokens = rms_back(tokens.astype(jnp.float32), factor, grad_normed).astype(jnp.bfloat16)
    return (grad_wkey, grad_wvalue, grad_tokens)

def latent_side(latents, key_rows, value_rows, live_slots, target, w_query, w_out, w_read):
    latent_rows, model_width = latents.shape
    head_dim = model_width // HEADS
    head_factor = head_dim ** (-0.5)
    query = matmul(latents, w_query).astype(jnp.bfloat16)
    query_heads = query.reshape(latent_rows, HEADS, head_dim)
    key_heads = key_rows.reshape(-1, HEADS, head_dim)
    value_heads = value_rows.reshape(-1, HEADS, head_dim)
    scores = contract('qhd,khd->hqk', query_heads, key_heads) * head_factor
    live_wide = live_slots[None, None, :]
    masked = jnp.where(live_wide, scores, -1e+30)
    row_max = lax.optimization_barrier(jnp.max(masked, axis=-1, keepdims=True))
    weights = jnp.where(live_wide, jnp.exp(masked - row_max), 0.0)
    probs = weights / lax.optimization_barrier(jnp.sum(weights, axis=-1, keepdims=True))
    probs_low = probs.astype(jnp.bfloat16)
    mixed_heads = contract('hqk,khd->qhd', probs_low, value_heads).reshape(latent_rows, model_width).astype(jnp.bfloat16)
    residual = latents.astype(jnp.float32) + matmul(mixed_heads, w_out)
    latent_factor = rms_scale(residual)
    normed = (residual * latent_factor).astype(jnp.bfloat16)
    logits = matmul(normed, w_read)
    grad_logits = ((jax.nn.sigmoid(logits) - target.astype(jnp.float32)) * latent_rows ** (-0.5)).astype(jnp.bfloat16)
    grad_wread = matmul(normed.T, grad_logits)
    grad_normed = matmul(grad_logits, w_read.T)
    grad_residual = rms_back(residual, latent_factor, grad_normed)
    grad_res_low = grad_residual.astype(jnp.bfloat16)
    grad_wout = matmul(mixed_heads.T, grad_res_low)
    grad_mixed = matmul(grad_res_low, w_out.T).astype(jnp.bfloat16).reshape(latent_rows, HEADS, head_dim)
    grad_probs = contract('qhd,khd->hqk', grad_mixed, value_heads)
    grad_values = contract('hqk,qhd->khd', probs_low, grad_mixed).reshape(-1, model_width).astype(jnp.bfloat16)
    inner = lax.optimization_barrier(jnp.sum(grad_probs * probs, axis=-1, keepdims=True))
    grad_scores = (probs * (grad_probs - inner) * head_factor).astype(jnp.bfloat16)
    grad_query = contract('hqk,khd->qhd', grad_scores, key_heads).reshape(latent_rows, model_width).astype(jnp.bfloat16)
    grad_keys = contract('hqk,qhd->khd', grad_scores, query_heads).reshape(-1, model_width).astype(jnp.bfloat16)
    grad_wquery = matmul(latents.T, grad_query)
    grad_latents = grad_residual + matmul(grad_query, w_query.T)
    return (grad_keys, grad_values, grad_wquery, grad_wout, grad_wread, grad_latents)

def reference(unit_ids, session_ids, counts, targets, unit_table, session_table, attn_weights, read_weight, latents):
    owners, sources, dests, slot_count = unit_ids.shape
    windows = owners * dests
    model_width = unit_table.shape[1]
    unit_windows = jnp.transpose(unit_ids, (0, 2, 1, 3)).reshape(windows, sources, slot_count)
    session_windows = jnp.transpose(session_ids, (0, 2, 1, 3)).reshape(windows, sources, slot_count)
    count_windows = jnp.transpose(counts, (0, 2, 1)).reshape(windows, sources)
    target_windows = targets.reshape(windows, targets.shape[2], targets.shape[3])
    w_query, w_key, w_value, w_out = (attn_weights[0], attn_weights[1], attn_weights[2], attn_weights[3])

    def window_step(carry, items):
        unit_rows, session_rows, got_counts, target = items
        tokens = (unit_table[unit_rows].astype(jnp.float32) + session_table[session_rows].astype(jnp.float32)).astype(jnp.bfloat16)
        tokens = tokens.reshape(sources * slot_count, model_width)
        live_slots = (jnp.arange(slot_count, dtype=jnp.int32)[None, :] < got_counts[:, None]).reshape(-1)
        normed, factor, key_rows, value_rows = event_front(tokens, w_key, w_value)
        grad_keys, grad_values, grad_wquery, grad_wout, grad_wread, grad_lat = latent_side(latents, key_rows, value_rows, live_slots, target, w_query, w_out, read_weight)
        grad_wkey, grad_wvalue, grad_tokens = event_back(tokens, factor, normed, grad_keys, grad_values, w_key, w_value)
        sum_attn, sum_read, sum_latents = carry
        sum_attn = sum_attn + jnp.stack([grad_wquery, grad_wkey, grad_wvalue, grad_wout])
        new_carry = (sum_attn, sum_read + grad_wread, sum_latents + grad_lat)
        return (new_carry, grad_tokens.reshape(sources, slot_count, model_width))
    start = (jnp.zeros(attn_weights.shape, jnp.float32), jnp.zeros(read_weight.shape, jnp.float32), jnp.zeros(latents.shape, jnp.float32))
    sums, event_rows = lax.scan(window_step, start, (unit_windows, session_windows, count_windows, target_windows))
    event_grad = event_rows.reshape(owners, dests, sources, slot_count, model_width)
    event_grad = jnp.transpose(event_grad, (0, 2, 1, 3, 4))
    return (event_grad, sums[0], sums[1], sums[2])
```

```python
import functools

import jax
import jax.numpy as jnp
from jax import lax
from jax.experimental import pallas as pl
from jax.experimental.pallas import tpu as pltpu
from jax.sharding import PartitionSpec as P

HEADS = 16
MESH = pl.DeviceIdType.MESH
MIB = 1 << 20


def flip(index, mask):
    out, bit = index, 1
    while bit <= mask:
        if mask & bit:
            out = out + bit - 2 * bit * lax.rem(lax.div(index, bit), 2)
        bit *= 2
    return out


def bit_orders(n_dp):
    bits = n_dp.bit_length() - 1
    high = [1 << b for b in range(bits - 1, 0, -1)]
    return (high + [1], high[::-1] + [1])


def masks_of(bits):
    out = [0]
    for bit in bits:
        out = out + [mask | bit for mask in out]
    return out


def wait_for(dst, sem):
    pltpu.make_async_copy(dst, dst, sem).wait()


def greet(n_dp, n_f):
    me, mine = lax.axis_index("dp"), lax.axis_index("fsdp")
    barrier = pltpu.get_barrier_semaphore()
    for k in range(1, n_dp):
        pl.semaphore_signal(
            barrier, inc=1, device_id={"dp": lax.rem(me + k, n_dp)}, device_id_type=MESH
        )
    for k in range(1, n_f):
        pl.semaphore_signal(
            barrier, inc=1, device_id={"fsdp": lax.rem(mine + k, n_f)}, device_id_type=MESH
        )
    pl.semaphore_wait(barrier, n_dp + n_f - 2)


def exchange_start(n_dp, src, dst, send, recv, local):
    me = lax.axis_index("dp")
    copies = []
    for k in range(1, n_dp):
        to = lax.rem(me + k, n_dp)
        copy = pltpu.make_async_remote_copy(
            src_ref=src.at[to],
            dst_ref=dst.at[me],
            send_sem=send.at[k],
            recv_sem=recv.at[k],
            device_id={"dp": to},
            device_id_type=MESH,
        )
        copy.start()
        copies.append(copy)
    own = pltpu.make_async_copy(src.at[me], dst.at[me], local)
    own.start()
    return copies, own


def exchange_finish(n_dp, started, dst, recv):
    me = lax.axis_index("dp")
    copies, own = started
    for k in range(1, n_dp):
        wait_for(dst.at[lax.rem(me + n_dp - k, n_dp)], recv.at[k])
    for copy in copies:
        copy.wait_send()
    own.wait()


def doubling(order, n_dp, half, buf, send, recv, ready):
    me = lax.axis_index("dp")
    held, copies, number = [0], [], 0
    for stage, bit in enumerate(order):
        for mask in held:
            if mask == 0:
                if stage == 0:
                    ready()
            elif mask & order[stage - 1]:
                wait_for(buf(flip(me, mask)), recv.at[half, mask])
            piece = buf(flip(me, mask))
            copy = pltpu.make_async_remote_copy(
                src_ref=piece,
                dst_ref=piece,
                send_sem=send.at[half, number],
                recv_sem=recv.at[half, mask | bit],
                device_id={"dp": flip(me, bit)},
                device_id_type=MESH,
            )
            copy.start()
            copies.append(copy)
            number += 1
        held = held + [mask | bit for mask in held]
        yield True
    for mask in held:
        if mask & order[-1]:
            wait_for(buf(flip(me, mask)), recv.at[half, mask])
    for copy in copies:
        copy.wait_send()


def staggered(walks):
    waiting, active = list(walks), []
    while waiting or active:
        if waiting:
            active.append(waiting.pop(0))
        still = []
        for walk in active:
            if next(walk, None) is not None:
                still.append(walk)
        active = still


def gather_kernel(n_dp, n_f, halves, ids, shard, got_ids, full, id_send, id_recv, z_send, send, recv, local):
    me, mine = lax.axis_index("dp"), lax.axis_index("fsdp")
    greet(n_dp, n_f)
    started = exchange_start(n_dp, ids, got_ids, id_send, id_recv, local.at[0])
    z_copies = []

    def send_over(half):
        for k in range(1, n_f):
            copy = pltpu.make_async_remote_copy(
                src_ref=shard.at[me, half],
                dst_ref=full.at[mine, me, half],
                send_sem=z_send.at[half, k],
                recv_sem=recv.at[n_f - k, half, 0],
                device_id={"fsdp": lax.rem(mine + k, n_f)},
                device_id_type=MESH,
            )
            copy.start()
            z_copies.append(copy)

    for half in range(min(2, halves)):
        send_over(half)
    own = pltpu.make_async_copy(shard, full.at[mine], local.at[1])
    own.start()
    orders = bit_orders(n_dp)

    def lane(half):
        walks = []
        for r in range(1, n_f):
            owner = lax.rem(mine + r, n_f)

            def buf(d, owner=owner):
                return full.at[owner, d, half]

            def ready(buf=buf, r=r):
                wait_for(buf(me), recv.at[r, half, 0])

            walks.append(
                doubling(orders[half % 2], n_dp, half, buf, send.at[r], recv.at[r], ready)
            )
        if half + 2 < halves:
            send_over(half + 2)
        for _ in orders[half % 2]:
            for walk in walks:
                next(walk)
            yield True
        for walk in walks:
            next(walk, None)

    staggered([lane(half) for half in range(halves)])
    for copy in z_copies:
        copy.wait_send()
    own.wait()
    exchange_finish(n_dp, started, got_ids, id_recv)


def gather_params(n_dp, n_f, ids, shard):
    halves = shard.shape[1]
    return pl.pallas_call(
        functools.partial(gather_kernel, n_dp, n_f, halves),
        out_shape=(
            jax.ShapeDtypeStruct(ids.shape, ids.dtype),
            jax.ShapeDtypeStruct((n_f,) + shard.shape, shard.dtype),
        ),
        in_specs=[pl.BlockSpec(memory_space=pltpu.VMEM)] * 2,
        out_specs=[pl.BlockSpec(memory_space=pltpu.VMEM)] * 2,
        scratch_shapes=[
            pltpu.SemaphoreType.DMA((n_dp,)),
            pltpu.SemaphoreType.DMA((n_dp,)),
            pltpu.SemaphoreType.DMA((halves, n_f)),
            pltpu.SemaphoreType.DMA((n_f, halves, n_dp)),
            pltpu.SemaphoreType.DMA((n_f, halves, n_dp)),
            pltpu.SemaphoreType.DMA((2,)),
        ],
        compiler_params=pltpu.CompilerParams(
            collective_id=0, has_side_effects=True, vmem_limit_bytes=40 * MIB
        ),
    )(ids, shard)


def halving(order, n_dp, half, grads, out_buf, in_buf, send, recv, load_sem):
    me = lax.axis_index("dp")
    n_f = grads.shape[0]
    bits, copies, number = order[::-1], [], 0
    pending, loaded = [], set()

    def load(mask):
        if mask not in loaded:
            loaded.add(mask)
            wait_for(grads.at[:, flip(me, mask), half], load_sem.at[half, mask])

    def add(slot, mask):
        load(mask)
        wait_for(in_buf.at[half, slot], recv.at[half, slot])
        where = flip(me, mask)
        for f in range(n_f):
            grads[f, where, half] += in_buf[half, slot, f].astype(jnp.float32)

    for stage, bit in enumerate(bits):
        rest = masks_of(bits[stage + 1:][::-1])
        rest = sorted(rest, key=lambda m: 0 if stage + 1 < len(bits) and m & bits[stage + 1] else 1)
        sends = [bit | m for m in rest]
        arrived = dict(pending)
        for mask in sends:
            if mask in arrived:
                add(arrived.pop(mask), mask)
            load(mask)
            slot = number
            number += 1
            where = flip(me, mask)
            for f in range(n_f):
                out_buf[half, slot, f] = grads[f, where, half].astype(jnp.bfloat16)
            copy = pltpu.make_async_remote_copy(
                src_ref=out_buf.at[half, slot],
                dst_ref=in_buf.at[half, slot],
                send_sem=send.at[half, slot],
                recv_sem=recv.at[half, slot],
                device_id={"dp": flip(me, bit)},
                device_id_type=MESH,
            )
            copy.start()
            copies.append(copy)
        yield True
        for mask, slot in arrived.items():
            add(slot, mask)
        pending = [(m, number - len(sends) + n) for n, m in enumerate(rest)]
    for mask, slot in pending:
        add(slot, mask)
    for copy in copies:
        copy.wait_send()


def reduce_kernel(
    n_dp, n_f, halves, source, events, summed, got_events, grads, out_buf, in_buf, z_out, z_in,
    load_sem, ev_send, ev_recv, h_send, h_recv, z_send, z_recv, d_send, d_recv, local,
):
    me, mine = lax.axis_index("dp"), lax.axis_index("fsdp")
    greet(n_dp, n_f)
    orders = bit_orders(n_dp)
    for half in range(halves):
        for mask in sorted(range(n_dp), key=lambda m: 0 if m & 1 else 1):
            where = flip(me, mask)
            pltpu.make_async_copy(
                source.at[:, where, half], grads.at[:, where, half], load_sem.at[half, mask]
            ).start()
    started = exchange_start(n_dp, events, got_events, ev_send, ev_recv, local.at[0])
    z_copies = []

    def lane(half):
        order = orders[half % 2]
        yield from halving(
            order, n_dp, half, grads, out_buf, in_buf, h_send, h_recv, load_sem
        )
        for k in range(1, n_f):
            to = lax.rem(mine + k, n_f)
            z_out[half, k] = grads[to, me, half].astype(jnp.bfloat16)
            copy = pltpu.make_async_remote_copy(
                src_ref=z_out.at[half, k],
                dst_ref=z_in.at[half, k],
                send_sem=z_send.at[half, k],
                recv_sem=z_recv.at[half, k],
                device_id={"fsdp": to},
                device_id_type=MESH,
            )
            copy.start()
            z_copies.append(copy)
        yield True

        def ready():
            total = grads[mine, me, half]
            for k in range(1, n_f):
                wait_for(z_in.at[half, k], z_recv.at[half, k])
                total = total + z_in[half, k].astype(jnp.float32)
            summed[me, half] = total.astype(jnp.bfloat16)

        def buf(d):
            return summed.at[d, half]

        yield from doubling(order, n_dp, half, buf, d_send, d_recv, ready)

    staggered([lane(half) for half in range(halves)])
    for copy in z_copies:
        copy.wait_send()
    exchange_finish(n_dp, started, got_events, ev_recv)


def reduce_grads(n_dp, n_f, grads, events):
    halves, rows, width = grads.shape[-3:]
    low = jnp.bfloat16
    return pl.pallas_call(
        functools.partial(reduce_kernel, n_dp, n_f, halves),
        out_shape=(
            jax.ShapeDtypeStruct(grads.shape[1:], low),
            jax.ShapeDtypeStruct(events.shape, low),
        ),
        in_specs=[pl.BlockSpec(memory_space=pl.ANY)] * 2,
        out_specs=[pl.BlockSpec(memory_space=pltpu.VMEM), pl.BlockSpec(memory_space=pl.ANY)],
        scratch_shapes=[
            pltpu.VMEM(grads.shape, jnp.float32),
            pltpu.VMEM((halves, n_dp - 1, n_f, rows, width), low),
            pltpu.VMEM((halves, n_dp - 1, n_f, rows, width), low),
            pltpu.VMEM((halves, n_f, rows, width), low),
            pltpu.VMEM((halves, n_f, rows, width), low),
            pltpu.SemaphoreType.DMA((halves, n_dp)),
            pltpu.SemaphoreType.DMA((n_dp,)),
            pltpu.SemaphoreType.DMA((n_dp,)),
            pltpu.SemaphoreType.DMA((halves, n_dp)),
            pltpu.SemaphoreType.DMA((halves, n_dp)),
            pltpu.SemaphoreType.DMA((halves, n_f)),
            pltpu.SemaphoreType.DMA((halves, n_f)),
            pltpu.SemaphoreType.DMA((halves, n_dp)),
            pltpu.SemaphoreType.DMA((halves, n_dp)),
            pltpu.SemaphoreType.DMA((1,)),
        ],
        compiler_params=pltpu.CompilerParams(
            collective_id=1, has_side_effects=True, vmem_limit_bytes=60 * MIB
        ),
    )(grads, events)


eps = 1e-05


def rms_scale(rows):
    return lax.rsqrt(jnp.mean(rows * rows, axis=-1, keepdims=True) + eps)


def rms_back(rows, factor, grad_out):
    cubed = factor * factor * factor
    return factor * grad_out - rows * cubed * jnp.mean(grad_out * rows, axis=-1, keepdims=True)


def dot_nn(left, right):
    return lax.dot_general(left, right, (((1,), (0,)), ((), ())), preferred_element_type=jnp.float32)


def dot_nt(left, right):
    return lax.dot_general(left, right, (((1,), (1,)), ((), ())), preferred_element_type=jnp.float32)


def dot_tn(left, right):
    return lax.dot_general(left, right, (((0,), (0,)), ((), ())), preferred_element_type=jnp.float32)


def window_kernel(
    sizes, slots, full, unit_table, session_table, target, grads, grad_tokens,
    tokens, normed, keys, values, query, mixed, gmixed, gquery, gkeys, gvalues, lat, lnorm, peak, scale,
    resid, ring, sems,
):
    n_f, own, read_rows, lat_rows, out_width = sizes
    width = tokens.shape[1]
    low = jnp.bfloat16
    base_read = 4 * own
    base_lat = base_read + read_rows
    end = base_lat + lat_rows
    times = width // out_width
    W_Q, W_K, W_V, W_O = range(4)
    state = {"n": 0, "busy": [None] * ring.shape[0]}

    def put(f, row, value):
        slot = state["n"] % ring.shape[0]
        state["n"] += 1
        if state["busy"][slot] is not None:
            state["busy"][slot].wait()
        rows = value.shape[0]
        ring[slot, pl.ds(0, rows)] = value
        copy = pltpu.make_async_copy(
            ring.at[slot, pl.ds(0, rows)], grads.at[f, pl.ds(row, rows)], sems.at[slot]
        )
        copy.start()
        state["busy"][slot] = copy

    def cols(f):
        return slice(f * own, (f + 1) * own)

    def block(k, f):
        return full[f, k * own:(k + 1) * own]

    def times_weight(left, k):
        total = dot_nn(left[:, cols(0)], block(k, 0))
        for f in range(1, n_f):
            total = total + dot_nn(left[:, cols(f)], block(k, f))
        return total

    def grad_matrix(left, right, k):
        for f in range(n_f):
            put(f, k * own, dot_tn(left[:, cols(f)], right[...]))

    slots_unit, slots_session, live = slots[0:1], slots[1:2], slots[2:3] > 0
    events = tokens.shape[0]

    def pick(table, ids, start, count):
        at = lax.broadcasted_iota(jnp.int32, (count, events), 0) + start
        return dot_tn((at == ids).astype(low), table[start:start + count])

    unit_rows = unit_table.shape[0]
    step = min(512, unit_rows)
    total = pick(unit_table, slots_unit, 0, step)
    for start in range(step, unit_rows, step):
        total = total + pick(unit_table, slots_unit, start, min(step, unit_rows - start))
    total = total + pick(session_table, slots_session, 0, session_table.shape[0])
    tokens[...] = total.astype(low)
    rows = tokens[...].astype(jnp.float32)
    normed[...] = (rows * rms_scale(rows)).astype(low)
    keys[...] = times_weight(normed, W_K).astype(low)
    values[...] = times_weight(normed, W_V).astype(low)
    for f in range(n_f):
        lat[f * lat_rows:(f + 1) * lat_rows] = full[f, base_lat:end]
    query[...] = times_weight(lat, W_Q).astype(low)

    latent_count = lat.shape[0]
    head_dim = width // HEADS
    head_factor = head_dim ** (-0.5)
    pack = 128 // head_dim
    which = lax.broadcasted_iota(jnp.int32, (1, 128), 1) // head_dim

    def masked(rows, part):
        return jnp.where(which == part, rows, jnp.zeros_like(rows))

    def merge(parts):
        out = parts[0]
        for part in range(1, pack):
            out = jnp.where(which == part, parts[part], out)
        return out

    def lanes(p):
        return pl.ds(pl.multiple_of(p * 128, 128), 128)

    def scores_of(q, k, part):
        return jnp.where(live, dot_nt(masked(q, part), k) * head_factor, -1e30)

    def forward(p, carry):
        q, k, v = query[:, lanes(p)], keys[:, lanes(p)], values[:, lanes(p)]
        outs = []
        for part in range(pack):
            s = scores_of(q, k, part)
            top = jnp.max(s, axis=-1, keepdims=True)
            w = jnp.where(live, jnp.exp(s - top), 0.0)
            inverse = 1.0 / jnp.sum(w, axis=-1, keepdims=True)
            peak[p * pack + part] = top
            scale[p * pack + part] = inverse
            outs.append(dot_nn((w * inverse).astype(low), v))
        mixed[:, lanes(p)] = merge(outs).astype(low)
        return carry

    lax.fori_loop(0, width // 128, forward, 0)

    resid[...] = lat[...].astype(jnp.float32) + times_weight(mixed, W_O)
    factor = rms_scale(resid[...])
    lnorm[...] = (resid[...] * factor).astype(low)

    def pieces():
        step = own // times
        for f in range(n_f):
            for t in range(times):
                at = f * own + t * step
                yield f, t, slice(at, at + step), full[f, base_read:base_lat, t * out_width:(t + 1) * out_width]

    logits = None
    for f, t, at, weight in pieces():
        term = dot_nn(lnorm[:, at], weight)
        logits = term if logits is None else logits + term
    glogits = (
        (jax.nn.sigmoid(logits) - target[...].astype(jnp.float32)) * latent_count ** (-0.5)
    ).astype(low)
    for f in range(n_f):
        put(f, base_read, jnp.concatenate(
            [dot_tn(lnorm[:, at], glogits) for g, t, at, _ in pieces() if g == f], axis=1
        ))
    glnorm = jnp.concatenate([dot_nt(glogits, weight) for _, _, _, weight in pieces()], axis=1)
    gresid = rms_back(resid[...], factor, glnorm)
    resid[...] = gresid
    gresid_low = gresid.astype(low)
    for f in range(n_f):
        gmixed[:, cols(f)] = dot_nt(gresid_low, block(W_O, f)).astype(low)
    lnorm[...] = gresid_low
    grad_matrix(mixed, lnorm, W_O)

    def backward(p, carry):
        q, k, v, g = query[:, lanes(p)], keys[:, lanes(p)], values[:, lanes(p)], gmixed[:, lanes(p)]
        outs = ([], [], [])
        for part in range(pack):
            s = scores_of(q, k, part)
            probs = jnp.where(live, jnp.exp(s - peak[p * pack + part]), 0.0) * scale[p * pack + part]
            gprobs = dot_nt(masked(g, part), v)
            inner = jnp.sum(gprobs * probs, axis=-1, keepdims=True)
            gscores = (probs * (gprobs - inner) * head_factor).astype(low)
            outs[0].append(dot_tn(probs.astype(low), g))
            outs[1].append(dot_nn(gscores, k))
            outs[2].append(dot_tn(gscores, q))
        gvalues[:, lanes(p)] = merge(outs[0]).astype(low)
        gquery[:, lanes(p)] = merge(outs[1]).astype(low)
        gkeys[:, lanes(p)] = merge(outs[2]).astype(low)
        return carry

    lax.fori_loop(0, width // 128, backward, 0)

    grad_matrix(lat, gquery, W_Q)
    for f in range(n_f):
        resid[:, cols(f)] += dot_nt(gquery[...], block(W_Q, f))
    for f in range(n_f):
        put(f, base_lat, resid[f * lat_rows:(f + 1) * lat_rows])
    grad_matrix(normed, gkeys, W_K)
    grad_matrix(normed, gvalues, W_V)
    spare = grads.shape[1] - end
    if spare:
        for f in range(n_f):
            put(f, end, jnp.zeros((spare, width), jnp.float32))
    gnormed = jnp.concatenate(
        [
            dot_nt(gkeys[...], block(W_K, f)) + dot_nt(gvalues[...], block(W_V, f))
            for f in range(n_f)
        ],
        axis=1,
    )
    rows = tokens[...].astype(jnp.float32)
    grad_tokens[...] = rms_back(rows, rms_scale(rows), gnormed).astype(low)
    for copy in state["busy"]:
        if copy is not None:
            copy.wait()


def window_grads(sizes, slots, full, unit_table, session_table, target):
    n_f, own, read_rows, lat_rows, out_width = sizes
    events, width = slots.shape[1], full.shape[-1]
    latent_count = n_f * lat_rows
    low = jnp.bfloat16
    spare = full.shape[1] - 4 * own - read_rows - lat_rows
    ring_rows = max(own, spare)
    by_event = pltpu.VMEM((events, width), low)
    by_latent = pltpu.VMEM((latent_count, width), low)
    column = pltpu.VMEM((HEADS, latent_count, 1), jnp.float32)
    return pl.pallas_call(
        functools.partial(window_kernel, sizes),
        out_shape=(
            jax.ShapeDtypeStruct(full.shape, jnp.float32),
            jax.ShapeDtypeStruct((events, width), low),
        ),
        in_specs=[pl.BlockSpec(memory_space=pltpu.VMEM)] * 5,
        out_specs=[pl.BlockSpec(memory_space=pl.ANY), pl.BlockSpec(memory_space=pltpu.VMEM)],
        scratch_shapes=[
            by_event, by_event, by_event, by_event,
            by_latent, by_latent, by_latent, by_latent,
            by_event, by_event, by_latent, by_latent, column, column,
            pltpu.VMEM((latent_count, width), jnp.float32),
            pltpu.VMEM((4, ring_rows, width), jnp.float32),
            pltpu.SemaphoreType.DMA((4,)),
        ],
        compiler_params=pltpu.CompilerParams(vmem_limit_bytes=60 * MIB),
    )(slots, full, unit_table, session_table, target)


def piece_rows(rows, n_dp):
    options = []
    for lanes in range(1, 6):
        lane_rows = -(-rows // (n_dp * lanes * 16)) * 16
        options.append((lane_rows * lanes, -lanes, lane_rows))
    _, lanes, lane_rows = min(options)
    return lane_rows, -lanes


def fold(rows, width):
    times = width // rows.shape[-1]
    step = rows.shape[-2] // times
    return jnp.concatenate(
        [rows[..., k * step:(k + 1) * step, :] for k in range(times)], axis=-1
    )


def unfold(rows, narrow):
    times = rows.shape[-1] // narrow
    return jnp.concatenate(
        [rows[..., k * narrow:(k + 1) * narrow] for k in range(times)], axis=-2
    )


def on_device(
    unit_ids,
    session_ids,
    counts,
    targets,
    unit_table,
    session_table,
    attn_weights,
    read_weight,
    latents,
):
    n_dp, n_f = lax.axis_size("dp"), lax.axis_size("fsdp")
    slot_count = unit_ids.shape[-1]
    width = unit_table.shape[1]
    event_total = n_dp * slot_count
    stack, own_rows, _ = attn_weights.shape
    read_rows = read_weight.size // width
    lat_rows = latents.shape[0]
    out_width = read_weight.shape[1]
    ends = (stack * own_rows, stack * own_rows + read_rows, stack * own_rows + read_rows + lat_rows)
    rows, halves = piece_rows(ends[2], n_dp)
    padded = rows * halves * n_dp

    id_rows = jnp.concatenate(
        [
            unit_ids.reshape(n_dp, slot_count),
            session_ids.reshape(n_dp, slot_count),
            (jnp.arange(slot_count, dtype=jnp.int32) < counts.reshape(n_dp, 1)).astype(jnp.int32),
        ],
        axis=1,
    )
    id_rows = jnp.pad(id_rows, ((0, 0), (0, 128 - id_rows.shape[1]))).reshape(n_dp, 1, 128)
    shard = jnp.concatenate(
        [
            attn_weights.reshape(stack * own_rows, width),
            fold(read_weight, width),
            latents,
            jnp.zeros((padded - ends[2], width), jnp.bfloat16),
        ]
    ).reshape(n_dp, halves, rows, width)
    got_ids, full = gather_params(n_dp, n_f, id_rows, shard)
    full = full.reshape(n_f, padded, width)
    sizes = (n_f, own_rows, read_rows, lat_rows, out_width)
    slots = jnp.transpose(got_ids[:, 0, :3 * slot_count].reshape(n_dp, 3, slot_count), (1, 0, 2))
    grads, grad_tokens = window_grads(
        sizes,
        slots.reshape(3, event_total),
        full,
        unit_table,
        session_table,
        targets.reshape(targets.shape[-2], out_width),
    )
    grads = grads.reshape(n_f, n_dp, halves, rows, width)
    summed, event_grad = reduce_grads(
        n_dp, n_f, grads, grad_tokens.reshape(n_dp, slot_count, width)
    )
    summed = summed.reshape(padded, width)
    return (
        event_grad.reshape(unit_ids.shape + (width,)),
        summed[:ends[0]].reshape(stack, own_rows, width).astype(jnp.float32),
        unfold(summed[ends[0]:ends[1]], out_width).astype(jnp.float32),
        summed[ends[1]:ends[2]].astype(jnp.float32),
    )


def solution(mesh):
    placed = (
        P("fsdp", "dp", None, None),
        P("fsdp", "dp", None, None),
        P("fsdp", "dp", None),
        P("fsdp", "dp", None, None),
        P(),
        P(),
        P(None, "fsdp", None),
        P("fsdp", None),
        P("fsdp", None),
    )
    return jax.shard_map(
        on_device,
        mesh=mesh,
        in_specs=placed,
        out_specs=(
            P("fsdp", "dp", None, None, None),
            P(None, "fsdp", None),
            P("fsdp", None),
            P("fsdp", None),
        ),
        check_vma=False,
    )
```

```python
import functools

import jax
import jax.numpy as jnp
from jax import lax
from jax.experimental import pallas as pl
from jax.experimental.pallas import tpu as pltpu
from jax.sharding import PartitionSpec as P

HEADS = 16
MESH = pl.DeviceIdType.MESH
MIB = 1 << 20


def flip(index, mask):
    out, bit = index, 1
    while bit <= mask:
        if mask & bit:
            out = out + bit - 2 * bit * lax.rem(lax.div(index, bit), 2)
        bit *= 2
    return out


def bit_orders(n_dp):
    bits = n_dp.bit_length() - 1
    high = [1 << b for b in range(bits - 1, 0, -1)]
    return (high + [1], high[::-1] + [1])


def masks_of(bits):
    out = [0]
    for bit in bits:
        out = out + [mask | bit for mask in out]
    return out


def wait_for(dst, sem):
    pltpu.make_async_copy(dst, dst, sem).wait()


def greet(n_dp, n_f):
    me, mine = lax.axis_index("dp"), lax.axis_index("fsdp")
    barrier = pltpu.get_barrier_semaphore()
    for k in range(1, n_dp):
        pl.semaphore_signal(
            barrier, inc=1, device_id={"dp": lax.rem(me + k, n_dp)}, device_id_type=MESH
        )
    for k in range(1, n_f):
        pl.semaphore_signal(
            barrier, inc=1, device_id={"fsdp": lax.rem(mine + k, n_f)}, device_id_type=MESH
        )
    pl.semaphore_wait(barrier, n_dp + n_f - 2)


def exchange_start(n_dp, src, dst, send, recv, local):
    me = lax.axis_index("dp")
    copies = []
    for k in range(1, n_dp):
        to = lax.rem(me + k, n_dp)
        copy = pltpu.make_async_remote_copy(
            src_ref=src.at[to],
            dst_ref=dst.at[me],
            send_sem=send.at[k],
            recv_sem=recv.at[k],
            device_id={"dp": to},
            device_id_type=MESH,
        )
        copy.start()
        copies.append(copy)
    own = pltpu.make_async_copy(src.at[me], dst.at[me], local)
    own.start()
    return copies, own


def exchange_finish(n_dp, started, dst, recv):
    me = lax.axis_index("dp")
    copies, own = started
    for k in range(1, n_dp):
        wait_for(dst.at[lax.rem(me + n_dp - k, n_dp)], recv.at[k])
    for copy in copies:
        copy.wait_send()
    own.wait()


def doubling(order, n_dp, half, buf, send, recv, ready):
    me = lax.axis_index("dp")
    held, copies, number = [0], [], 0
    for stage, bit in enumerate(order):
        for mask in held:
            if mask == 0:
                if stage == 0:
                    ready()
            elif mask & order[stage - 1]:
                wait_for(buf(flip(me, mask)), recv.at[half, mask])
            piece = buf(flip(me, mask))
            copy = pltpu.make_async_remote_copy(
                src_ref=piece,
                dst_ref=piece,
                send_sem=send.at[half, number],
                recv_sem=recv.at[half, mask | bit],
                device_id={"dp": flip(me, bit)},
                device_id_type=MESH,
            )
            copy.start()
            copies.append(copy)
            number += 1
        held = held + [mask | bit for mask in held]
        yield True
    for mask in held:
        if mask & order[-1]:
            wait_for(buf(flip(me, mask)), recv.at[half, mask])
    for copy in copies:
        copy.wait_send()


def staggered(walks):
    waiting, active = list(walks), []
    while waiting or active:
        if waiting:
            active.append(waiting.pop(0))
        still = []
        for walk in active:
            if next(walk, None) is not None:
                still.append(walk)
        active = still
        yield True


def gather(n_dp, n_f, halves, lane_rows, full, z_send, send, recv):
    me, mine = lax.axis_index("dp"), lax.axis_index("fsdp")
    z_copies, done = [], set()
    orders = bit_orders(n_dp)

    def at(d, half):
        return pl.ds(pl.multiple_of((half * n_dp + d) * lane_rows, 16), lane_rows)

    def send_over(half):
        for k in range(1, n_f):
            piece = full.at[mine, at(me, half)]
            copy = pltpu.make_async_remote_copy(
                src_ref=piece,
                dst_ref=piece,
                send_sem=z_send.at[half, k],
                recv_sem=recv.at[n_f - k, half, 0],
                device_id={"fsdp": lax.rem(mine + k, n_f)},
                device_id_type=MESH,
            )
            copy.start()
            z_copies.append(copy)

    for half in range(min(2, halves)):
        send_over(half)

    def lane(half):
        walks = []
        for r in range(1, n_f):
            owner = lax.rem(mine + r, n_f)

            def buf(d, owner=owner):
                return full.at[owner, at(d, half)]

            def ready(buf=buf, r=r):
                wait_for(buf(me), recv.at[r, half, 0])

            walks.append(
                doubling(orders[half % 2], n_dp, half, buf, send.at[r], recv.at[r], ready)
            )
        if half + 2 < halves:
            send_over(half + 2)
        for _ in orders[half % 2]:
            for walk in walks:
                next(walk)
            yield True
        for walk in walks:
            next(walk, None)
        done.add(half)

    progress = staggered([lane(half) for half in range(halves)])

    def need(stop):
        last = -(-stop // (n_dp * lane_rows)) - 1
        while not all(half in done for half in range(last + 1)):
            next(progress)

    def end():
        for _ in progress:
            pass
        for copy in z_copies:
            copy.wait_send()

    return progress, need, end


def halving(order, n_dp, half, grads, out_buf, in_buf, send, recv, load_sem):
    me = lax.axis_index("dp")
    n_f = grads.shape[0]
    bits, copies, number = order[::-1], [], 0
    pending, loaded = [], set()

    def load(mask):
        if mask not in loaded:
            loaded.add(mask)
            wait_for(grads.at[:, flip(me, mask), half], load_sem.at[half, mask])

    def add(slot, mask):
        load(mask)
        wait_for(in_buf.at[half, slot], recv.at[half, slot])
        where = flip(me, mask)
        for f in range(n_f):
            grads[f, where, half] += in_buf[half, slot, f].astype(jnp.float32)

    for stage, bit in enumerate(bits):
        rest = masks_of(bits[stage + 1:][::-1])
        rest = sorted(rest, key=lambda m: 0 if stage + 1 < len(bits) and m & bits[stage + 1] else 1)
        sends = [bit | m for m in rest]
        arrived = dict(pending)
        for mask in sends:
            if mask in arrived:
                add(arrived.pop(mask), mask)
            load(mask)
            slot = number
            number += 1
            where = flip(me, mask)
            for f in range(n_f):
                out_buf[half, slot, f] = grads[f, where, half].astype(jnp.bfloat16)
            copy = pltpu.make_async_remote_copy(
                src_ref=out_buf.at[half, slot],
                dst_ref=in_buf.at[half, slot],
                send_sem=send.at[half, slot],
                recv_sem=recv.at[half, slot],
                device_id={"dp": flip(me, bit)},
                device_id_type=MESH,
            )
            copy.start()
            copies.append(copy)
        yield True
        for mask, slot in arrived.items():
            add(slot, mask)
        pending = [(m, number - len(sends) + n) for n, m in enumerate(rest)]
    for mask, slot in pending:
        add(slot, mask)
    for copy in copies:
        copy.wait_send()


def reduce_kernel(
    n_dp, n_f, halves, source, events, summed, got_events, grads, out_buf, in_buf, z_out, z_in,
    load_sem, ev_send, ev_recv, h_send, h_recv, z_send, z_recv, d_send, d_recv, local,
):
    me, mine = lax.axis_index("dp"), lax.axis_index("fsdp")
    greet(n_dp, n_f)
    orders = bit_orders(n_dp)
    for half in range(halves):
        for mask in sorted(range(n_dp), key=lambda m: 0 if m & 1 else 1):
            where = flip(me, mask)
            pltpu.make_async_copy(
                source.at[:, where, half], grads.at[:, where, half], load_sem.at[half, mask]
            ).start()
    started = exchange_start(n_dp, events, got_events, ev_send, ev_recv, local.at[0])
    z_copies = []

    def lane(half):
        order = orders[half % 2]
        yield from halving(
            order, n_dp, half, grads, out_buf, in_buf, h_send, h_recv, load_sem
        )
        for k in range(1, n_f):
            to = lax.rem(mine + k, n_f)
            z_out[half, k] = grads[to, me, half].astype(jnp.bfloat16)
            copy = pltpu.make_async_remote_copy(
                src_ref=z_out.at[half, k],
                dst_ref=z_in.at[half, k],
                send_sem=z_send.at[half, k],
                recv_sem=z_recv.at[half, k],
                device_id={"fsdp": to},
                device_id_type=MESH,
            )
            copy.start()
            z_copies.append(copy)
        yield True

        def ready():
            total = grads[mine, me, half]
            for k in range(1, n_f):
                wait_for(z_in.at[half, k], z_recv.at[half, k])
                total = total + z_in[half, k].astype(jnp.float32)
            summed[me, half] = total.astype(jnp.bfloat16)

        def buf(d):
            return summed.at[d, half]

        yield from doubling(order, n_dp, half, buf, d_send, d_recv, ready)

    for _ in staggered([lane(half) for half in range(halves)]):
        pass
    for copy in z_copies:
        copy.wait_send()
    exchange_finish(n_dp, started, got_events, ev_recv)


def reduce_grads(n_dp, n_f, grads, events):
    halves, rows, width = grads.shape[-3:]
    low = jnp.bfloat16
    return pl.pallas_call(
        functools.partial(reduce_kernel, n_dp, n_f, halves),
        out_shape=(
            jax.ShapeDtypeStruct(grads.shape[1:], low),
            jax.ShapeDtypeStruct(events.shape, low),
        ),
        in_specs=[pl.BlockSpec(memory_space=pl.ANY)] * 2,
        out_specs=[pl.BlockSpec(memory_space=pltpu.VMEM), pl.BlockSpec(memory_space=pl.ANY)],
        scratch_shapes=[
            pltpu.VMEM(grads.shape, jnp.float32),
            pltpu.VMEM((halves, n_dp - 1, n_f, rows, width), low),
            pltpu.VMEM((halves, n_dp - 1, n_f, rows, width), low),
            pltpu.VMEM((halves, n_f, rows, width), low),
            pltpu.VMEM((halves, n_f, rows, width), low),
            pltpu.SemaphoreType.DMA((halves, n_dp)),
            pltpu.SemaphoreType.DMA((n_dp,)),
            pltpu.SemaphoreType.DMA((n_dp,)),
            pltpu.SemaphoreType.DMA((halves, n_dp)),
            pltpu.SemaphoreType.DMA((halves, n_dp)),
            pltpu.SemaphoreType.DMA((halves, n_f)),
            pltpu.SemaphoreType.DMA((halves, n_f)),
            pltpu.SemaphoreType.DMA((halves, n_dp)),
            pltpu.SemaphoreType.DMA((halves, n_dp)),
            pltpu.SemaphoreType.DMA((1,)),
        ],
        compiler_params=pltpu.CompilerParams(
            collective_id=1, has_side_effects=True, vmem_limit_bytes=60 * MIB
        ),
    )(grads, events)


eps = 1e-05


def rms_scale(rows):
    return lax.rsqrt(jnp.mean(rows * rows, axis=-1, keepdims=True) + eps)


def rms_back(rows, factor, grad_out):
    cubed = factor * factor * factor
    return factor * grad_out - rows * cubed * jnp.mean(grad_out * rows, axis=-1, keepdims=True)


def dot_nn(left, right):
    return lax.dot_general(left, right, (((1,), (0,)), ((), ())), preferred_element_type=jnp.float32)


def dot_nt(left, right):
    return lax.dot_general(left, right, (((1,), (1,)), ((), ())), preferred_element_type=jnp.float32)


def dot_tn(left, right):
    return lax.dot_general(left, right, (((0,), (0,)), ((), ())), preferred_element_type=jnp.float32)


def window_kernel(
    grid, sizes, ids, attn, read, latents, unit_table, session_table, target, grads, grad_tokens,
    got_ids, full, id_send, id_recv, z_send, send, recv, local,
    tokens, normed, keys, values, query, mixed, gmixed, gquery, gkeys, gvalues, lat, lnorm, peak, scale,
    resid, ring, sems,
):
    n_dp, n_f, halves, lane_rows, slot_count = grid
    n_f, own, read_rows, lat_rows, out_width = sizes
    mine = lax.axis_index("fsdp")
    width = tokens.shape[1]
    low = jnp.bfloat16
    base_read = 4 * own
    base_lat = base_read + read_rows
    end = base_lat + lat_rows
    times = width // out_width
    W_Q, W_K, W_V, W_O = range(4)
    padded = full.shape[1]
    place = (padded - 2 * own, 0, own, padded - own)
    at_lat = 2 * own
    at_read = at_lat + lat_rows
    filled = at_read + read_rows

    moves = [(attn.at[k], full.at[mine, pl.ds(place[k], own)]) for k in range(4)]
    moves.append((latents, full.at[mine, pl.ds(at_lat, lat_rows)]))
    for t in range(times):
        moves.append((
            read.at[pl.ds(t * read_rows, read_rows)],
            full.at[mine, pl.ds(at_read, read_rows), pl.ds(t * out_width, out_width)],
        ))
    moves = [pltpu.make_async_copy(src, dst, local.at[1 + n]) for n, (src, dst) in enumerate(moves)]
    for move in moves:
        move.start()
    if filled < place[W_Q]:
        full[mine, filled:place[W_Q]] = jnp.zeros((place[W_Q] - filled, width), low)
    greet(n_dp, n_f)
    started = exchange_start(n_dp, ids, got_ids, id_send, id_recv, local.at[0])
    for move in moves:
        move.wait()
    progress, need, end_gather = gather(n_dp, n_f, halves, lane_rows, full, z_send, send, recv)
    exchange_finish(n_dp, started, got_ids, id_recv)
    state = {"n": 0, "busy": [None] * ring.shape[0]}

    def put(f, row, value):
        slot = state["n"] % ring.shape[0]
        state["n"] += 1
        if state["busy"][slot] is not None:
            state["busy"][slot].wait()
        rows = value.shape[0]
        ring[slot, pl.ds(0, rows)] = value
        copy = pltpu.make_async_copy(
            ring.at[slot, pl.ds(0, rows)], grads.at[f, pl.ds(row, rows)], sems.at[slot]
        )
        copy.start()
        state["busy"][slot] = copy

    def cols(f):
        return slice(f * own, (f + 1) * own)

    def block(k, f):
        return full[f, place[k]:place[k] + own]

    def times_weight(left, k):
        total = dot_nn(left[:, cols(0)], block(k, 0))
        for f in range(1, n_f):
            total = total + dot_nn(left[:, cols(f)], block(k, f))
        return total

    def grad_matrix(left, right, k):
        for f in range(n_f):
            put(f, k * own, dot_tn(left[:, cols(f)], right[...]))

    def slots(k):
        return jnp.concatenate(
            [got_ids[d, :, k * slot_count:(k + 1) * slot_count] for d in range(n_dp)], axis=1
        )

    slots_unit, slots_session, live = slots(0), slots(1), slots(2) > 0
    events = tokens.shape[0]

    def pick(table, ids, start, count):
        at = lax.broadcasted_iota(jnp.int32, (count, events), 0) + start
        return dot_tn((at == ids).astype(low), table[start:start + count])

    unit_rows = unit_table.shape[0]
    step = min(512, unit_rows)
    total = pick(unit_table, slots_unit, 0, step)
    for start in range(step, unit_rows, step):
        total = total + pick(unit_table, slots_unit, start, min(step, unit_rows - start))
    total = total + pick(session_table, slots_session, 0, session_table.shape[0])
    tokens[...] = total.astype(low)
    rows = tokens[...].astype(jnp.float32)
    normed[...] = (rows * rms_scale(rows)).astype(low)
    need(own)
    keys[...] = times_weight(normed, W_K).astype(low)
    need(2 * own)
    values[...] = times_weight(normed, W_V).astype(low)
    need(place[W_Q] + own)
    for f in range(n_f):
        lat[f * lat_rows:(f + 1) * lat_rows] = full[f, at_lat:at_lat + lat_rows]
    query[...] = times_weight(lat, W_Q).astype(low)

    latent_count = lat.shape[0]
    head_dim = width // HEADS
    head_factor = head_dim ** (-0.5)
    pack = 128 // head_dim
    which = lax.broadcasted_iota(jnp.int32, (1, 128), 1) // head_dim

    def masked(rows, part):
        return jnp.where(which == part, rows, jnp.zeros_like(rows))

    def merge(parts):
        out = parts[0]
        for part in range(1, pack):
            out = jnp.where(which == part, parts[part], out)
        return out

    def lanes(p):
        return pl.ds(pl.multiple_of(p * 128, 128), 128)

    def scores_of(q, k, part):
        return jnp.where(live, dot_nt(masked(q, part), k) * head_factor, -1e30)

    def forward(p, carry):
        q, k, v = query[:, lanes(p)], keys[:, lanes(p)], values[:, lanes(p)]
        outs = []
        for part in range(pack):
            s = scores_of(q, k, part)
            top = jnp.max(s, axis=-1, keepdims=True)
            w = jnp.where(live, jnp.exp(s - top), 0.0)
            inverse = 1.0 / jnp.sum(w, axis=-1, keepdims=True)
            peak[p * pack + part] = top
            scale[p * pack + part] = inverse
            outs.append(dot_nn((w * inverse).astype(low), v))
        mixed[:, lanes(p)] = merge(outs).astype(low)
        return carry

    lax.fori_loop(0, width // 128, forward, 0)

    end_gather()
    resid[...] = lat[...].astype(jnp.float32) + times_weight(mixed, W_O)
    factor = rms_scale(resid[...])
    lnorm[...] = (resid[...] * factor).astype(low)

    def pieces():
        step = own // times
        for f in range(n_f):
            for t in range(times):
                at = f * own + t * step
                yield f, t, slice(at, at + step), full[f, at_read:filled, t * out_width:(t + 1) * out_width]

    logits = None
    for f, t, at, weight in pieces():
        term = dot_nn(lnorm[:, at], weight)
        logits = term if logits is None else logits + term
    glogits = (
        (jax.nn.sigmoid(logits) - target[...].astype(jnp.float32)) * latent_count ** (-0.5)
    ).astype(low)
    for f in range(n_f):
        put(f, base_read, jnp.concatenate(
            [dot_tn(lnorm[:, at], glogits) for g, t, at, _ in pieces() if g == f], axis=1
        ))
    glnorm = jnp.concatenate([dot_nt(glogits, weight) for _, _, _, weight in pieces()], axis=1)
    gresid = rms_back(resid[...], factor, glnorm)
    resid[...] = gresid
    gresid_low = gresid.astype(low)
    for f in range(n_f):
        gmixed[:, cols(f)] = dot_nt(gresid_low, block(W_O, f)).astype(low)
    lnorm[...] = gresid_low
    grad_matrix(mixed, lnorm, W_O)

    def backward(p, carry):
        q, k, v, g = query[:, lanes(p)], keys[:, lanes(p)], values[:, lanes(p)], gmixed[:, lanes(p)]
        outs = ([], [], [])
        for part in range(pack):
            s = scores_of(q, k, part)
            probs = jnp.where(live, jnp.exp(s - peak[p * pack + part]), 0.0) * scale[p * pack + part]
            gprobs = dot_nt(masked(g, part), v)
            inner = jnp.sum(gprobs * probs, axis=-1, keepdims=True)
            gscores = (probs * (gprobs - inner) * head_factor).astype(low)
            outs[0].append(dot_tn(probs.astype(low), g))
            outs[1].append(dot_nn(gscores, k))
            outs[2].append(dot_tn(gscores, q))
        gvalues[:, lanes(p)] = merge(outs[0]).astype(low)
        gquery[:, lanes(p)] = merge(outs[1]).astype(low)
        gkeys[:, lanes(p)] = merge(outs[2]).astype(low)
        return carry

    lax.fori_loop(0, width // 128, backward, 0)

    grad_matrix(lat, gquery, W_Q)
    for f in range(n_f):
        resid[:, cols(f)] += dot_nt(gquery[...], block(W_Q, f))
    for f in range(n_f):
        put(f, base_lat, resid[f * lat_rows:(f + 1) * lat_rows])
    grad_matrix(normed, gkeys, W_K)
    grad_matrix(normed, gvalues, W_V)
    spare = grads.shape[1] - end
    if spare:
        for f in range(n_f):
            put(f, end, jnp.zeros((spare, width), jnp.float32))
    gnormed = jnp.concatenate(
        [
            dot_nt(gkeys[...], block(W_K, f)) + dot_nt(gvalues[...], block(W_V, f))
            for f in range(n_f)
        ],
        axis=1,
    )
    rows = tokens[...].astype(jnp.float32)
    grad_tokens[...] = rms_back(rows, rms_scale(rows), gnormed).astype(low)
    for copy in state["busy"]:
        if copy is not None:
            copy.wait()


def window_grads(grid, sizes, ids, attn, read, latents, unit_table, session_table, target):
    n_dp, n_f, halves, lane_rows, slot_count = grid
    n_f, own, read_rows, lat_rows, out_width = sizes
    events, width = n_dp * slot_count, attn.shape[-1]
    latent_count = n_f * lat_rows
    low = jnp.bfloat16
    padded = halves * n_dp * lane_rows
    ring_rows = max(own, padded - 4 * own - read_rows - lat_rows)
    by_event = pltpu.VMEM((events, width), low)
    by_latent = pltpu.VMEM((latent_count, width), low)
    column = pltpu.VMEM((HEADS, latent_count, 1), jnp.float32)
    in_vmem, anywhere = pl.BlockSpec(memory_space=pltpu.VMEM), pl.BlockSpec(memory_space=pl.ANY)
    return pl.pallas_call(
        functools.partial(window_kernel, grid, sizes),
        out_shape=(
            jax.ShapeDtypeStruct((n_f, padded, width), jnp.float32),
            jax.ShapeDtypeStruct((events, width), low),
        ),
        in_specs=[in_vmem] + [anywhere] * 3 + [in_vmem] * 3,
        out_specs=[anywhere, in_vmem],
        scratch_shapes=[
            pltpu.VMEM(ids.shape, ids.dtype),
            pltpu.VMEM((n_f, padded, width), low),
            pltpu.SemaphoreType.DMA((n_dp,)),
            pltpu.SemaphoreType.DMA((n_dp,)),
            pltpu.SemaphoreType.DMA((halves, n_f)),
            pltpu.SemaphoreType.DMA((n_f, halves, n_dp)),
            pltpu.SemaphoreType.DMA((n_f, halves, n_dp)),
            pltpu.SemaphoreType.DMA((6 + width // out_width,)),
            by_event, by_event, by_event, by_event,
            by_latent, by_latent, by_latent, by_latent,
            by_event, by_event, by_latent, by_latent, column, column,
            pltpu.VMEM((latent_count, width), jnp.float32),
            pltpu.VMEM((4, ring_rows, width), jnp.float32),
            pltpu.SemaphoreType.DMA((4,)),
        ],
        compiler_params=pltpu.CompilerParams(
            collective_id=0, has_side_effects=True, vmem_limit_bytes=60 * MIB
        ),
    )(ids, attn, read, latents, unit_table, session_table, target)


def piece_rows(rows, n_dp):
    options = []
    for lanes in range(1, 6):
        lane_rows = -(-rows // (n_dp * lanes * 16)) * 16
        options.append((lane_rows * lanes, -lanes, lane_rows))
    _, lanes, lane_rows = min(options)
    return lane_rows, -lanes


def unfold(rows, narrow):
    times = rows.shape[-1] // narrow
    return jnp.concatenate(
        [rows[..., k * narrow:(k + 1) * narrow] for k in range(times)], axis=-2
    )


def on_device(
    unit_ids,
    session_ids,
    counts,
    targets,
    unit_table,
    session_table,
    attn_weights,
    read_weight,
    latents,
):
    n_dp, n_f = lax.axis_size("dp"), lax.axis_size("fsdp")
    slot_count = unit_ids.shape[-1]
    width = unit_table.shape[1]
    event_total = n_dp * slot_count
    stack, own_rows, _ = attn_weights.shape
    read_rows = read_weight.size // width
    lat_rows = latents.shape[0]
    out_width = read_weight.shape[1]
    ends = (stack * own_rows, stack * own_rows + read_rows, stack * own_rows + read_rows + lat_rows)
    rows, halves = piece_rows(ends[2], n_dp)
    padded = rows * halves * n_dp

    id_rows = jnp.concatenate(
        [
            unit_ids.reshape(n_dp, slot_count),
            session_ids.reshape(n_dp, slot_count),
            (jnp.arange(slot_count, dtype=jnp.int32) < counts.reshape(n_dp, 1)).astype(jnp.int32),
        ],
        axis=1,
    )
    id_rows = jnp.pad(id_rows, ((0, 0), (0, 128 - id_rows.shape[1]))).reshape(n_dp, 1, 128)
    grads, grad_tokens = window_grads(
        (n_dp, n_f, halves, rows, slot_count),
        (n_f, own_rows, read_rows, lat_rows, out_width),
        id_rows,
        attn_weights,
        read_weight,
        latents,
        unit_table,
        session_table,
        targets.reshape(targets.shape[-2], out_width),
    )
    grads = grads.reshape(n_f, n_dp, halves, rows, width)
    summed, event_grad = reduce_grads(
        n_dp, n_f, grads, grad_tokens.reshape(n_dp, slot_count, width)
    )
    summed = summed.reshape(padded, width)
    return (
        event_grad.reshape(unit_ids.shape + (width,)),
        summed[:ends[0]].reshape(stack, own_rows, width).astype(jnp.float32),
        unfold(summed[ends[0]:ends[1]], out_width).astype(jnp.float32),
        summed[ends[1]:ends[2]].astype(jnp.float32),
    )


def solution(mesh):
    placed = (
        P("fsdp", "dp", None, None),
        P("fsdp", "dp", None, None),
        P("fsdp", "dp", None),
        P("fsdp", "dp", None, None),
        P(),
        P(),
        P(None, "fsdp", None),
        P("fsdp", None),
        P("fsdp", None),
    )
    return jax.shard_map(
        on_device,
        mesh=mesh,
        in_specs=placed,
        out_specs=(
            P("fsdp", "dp", None, None, None),
            P(None, "fsdp", None),
            P("fsdp", None),
            P("fsdp", None),
        ),
        check_vma=False,
    )
```

```python
import functools

import jax
import jax.numpy as jnp
from jax import lax
from jax.experimental import pallas as pl
from jax.experimental.pallas import tpu as pltpu
from jax.sharding import PartitionSpec as P

HEADS = 16
MESH = pl.DeviceIdType.MESH
MIB = 1 << 20


def flip(index, mask):
    out, bit = index, 1
    while bit <= mask:
        if mask & bit:
            out = out + bit - 2 * bit * lax.rem(lax.div(index, bit), 2)
        bit *= 2
    return out


def bit_orders(n_dp):
    bits = n_dp.bit_length() - 1
    high = [1 << b for b in range(bits - 1, 0, -1)]
    return (high + [1], high[::-1] + [1])


def masks_of(bits):
    out = [0]
    for bit in bits:
        out = out + [mask | bit for mask in out]
    return out


def wait_for(dst, sem):
    pltpu.make_async_copy(dst, dst, sem).wait()


def greet(n_dp, n_f):
    me, mine = lax.axis_index("dp"), lax.axis_index("fsdp")
    barrier = pltpu.get_barrier_semaphore()
    for k in range(1, n_dp):
        pl.semaphore_signal(
            barrier, inc=1, device_id={"dp": lax.rem(me + k, n_dp)}, device_id_type=MESH
        )
    for k in range(1, n_f):
        pl.semaphore_signal(
            barrier, inc=1, device_id={"fsdp": lax.rem(mine + k, n_f)}, device_id_type=MESH
        )
    pl.semaphore_wait(barrier, n_dp + n_f - 2)


def exchange_start(n_dp, src, dst, send, recv, local):
    me = lax.axis_index("dp")
    copies = []
    for k in range(1, n_dp):
        to = lax.rem(me + k, n_dp)
        copy = pltpu.make_async_remote_copy(
            src_ref=src.at[to],
            dst_ref=dst.at[me],
            send_sem=send.at[k],
            recv_sem=recv.at[k],
            device_id={"dp": to},
            device_id_type=MESH,
        )
        copy.start()
        copies.append(copy)
    own = pltpu.make_async_copy(src.at[me], dst.at[me], local)
    own.start()
    return copies, own


def exchange_finish(n_dp, started, dst, recv):
    me = lax.axis_index("dp")
    copies, own = started
    for k in range(1, n_dp):
        wait_for(dst.at[lax.rem(me + n_dp - k, n_dp)], recv.at[k])
    for copy in copies:
        copy.wait_send()
    own.wait()


def doubling(order, n_dp, half, buf, send, recv, ready):
    me = lax.axis_index("dp")
    held, copies, number = [0], [], 0
    for stage, bit in enumerate(order):
        for mask in held:
            if mask == 0:
                if stage == 0:
                    ready()
            elif mask & order[stage - 1]:
                wait_for(buf(flip(me, mask)), recv.at[half, mask])
            piece = buf(flip(me, mask))
            copy = pltpu.make_async_remote_copy(
                src_ref=piece,
                dst_ref=piece,
                send_sem=send.at[half, number],
                recv_sem=recv.at[half, mask | bit],
                device_id={"dp": flip(me, bit)},
                device_id_type=MESH,
            )
            copy.start()
            copies.append(copy)
            number += 1
        held = held + [mask | bit for mask in held]
        yield True
    for mask in held:
        if mask & order[-1]:
            wait_for(buf(flip(me, mask)), recv.at[half, mask])
    for copy in copies:
        copy.wait_send()


def staggered(walks):
    waiting, active = list(walks), []
    while waiting or active:
        active, waiting = active + waiting[:2], waiting[2:]
        still = []
        for walk in active:
            if next(walk, None) is not None:
                still.append(walk)
        active = still
        yield True


def gather(n_dp, n_f, halves, lane_rows, full, z_send, send, recv):
    me, mine = lax.axis_index("dp"), lax.axis_index("fsdp")
    z_copies, done = [], set()
    orders = bit_orders(n_dp)

    def at(d, half):
        return pl.ds(pl.multiple_of((half * n_dp + d) * lane_rows, 16), lane_rows)

    def send_over(half):
        for k in range(1, n_f):
            piece = full.at[mine, at(me, half)]
            copy = pltpu.make_async_remote_copy(
                src_ref=piece,
                dst_ref=piece,
                send_sem=z_send.at[half, k],
                recv_sem=recv.at[n_f - k, half, 0],
                device_id={"fsdp": lax.rem(mine + k, n_f)},
                device_id_type=MESH,
            )
            copy.start()
            z_copies.append(copy)

    for half in range(min(2, halves)):
        send_over(half)

    def lane(half):
        walks = []
        for r in range(1, n_f):
            owner = lax.rem(mine + r, n_f)

            def buf(d, owner=owner):
                return full.at[owner, at(d, half)]

            def ready(buf=buf, r=r):
                wait_for(buf(me), recv.at[r, half, 0])

            walks.append(
                doubling(orders[half % 2], n_dp, half, buf, send.at[r], recv.at[r], ready)
            )
        if half + 2 < halves:
            send_over(half + 2)
        for _ in orders[half % 2]:
            for walk in walks:
                next(walk)
            yield True
        for walk in walks:
            next(walk, None)
        done.add(half)

    progress = staggered([lane(half) for half in range(halves)])

    def need(stop):
        last = -(-stop // (n_dp * lane_rows)) - 1
        while not all(half in done for half in range(last + 1)):
            next(progress)

    def end():
        for _ in progress:
            pass
        for copy in z_copies:
            copy.wait_send()

    return progress, need, end


def halving(order, n_dp, half, grads, out_buf, in_buf, send, recv, load_sem):
    me = lax.axis_index("dp")
    n_f = grads.shape[0]
    bits, copies, number = order[::-1], [], 0
    pending, loaded = [], set()

    def load(mask):
        if mask not in loaded:
            loaded.add(mask)
            wait_for(grads.at[:, flip(me, mask), half], load_sem.at[half, mask])

    def add(slot, mask):
        load(mask)
        wait_for(in_buf.at[half, slot], recv.at[half, slot])
        where = flip(me, mask)
        for f in range(n_f):
            grads[f, where, half] += in_buf[half, slot, f].astype(jnp.float32)

    for stage, bit in enumerate(bits):
        rest = masks_of(bits[stage + 1:][::-1])
        rest = sorted(rest, key=lambda m: 0 if stage + 1 < len(bits) and m & bits[stage + 1] else 1)
        sends = [bit | m for m in rest]
        arrived = dict(pending)
        for mask in sends:
            if mask in arrived:
                add(arrived.pop(mask), mask)
            load(mask)
            slot = number
            number += 1
            where = flip(me, mask)
            for f in range(n_f):
                out_buf[half, slot, f] = grads[f, where, half].astype(jnp.bfloat16)
            copy = pltpu.make_async_remote_copy(
                src_ref=out_buf.at[half, slot],
                dst_ref=in_buf.at[half, slot],
                send_sem=send.at[half, slot],
                recv_sem=recv.at[half, slot],
                device_id={"dp": flip(me, bit)},
                device_id_type=MESH,
            )
            copy.start()
            copies.append(copy)
        yield True
        for mask, slot in arrived.items():
            add(slot, mask)
        pending = [(m, number - len(sends) + n) for n, m in enumerate(rest)]
    for mask, slot in pending:
        add(slot, mask)
    for copy in copies:
        copy.wait_send()


def reduce_kernel(
    n_dp, n_f, halves, source, events, summed, got_events, grads, out_buf, in_buf, z_out, z_in,
    load_sem, ev_send, ev_recv, h_send, h_recv, z_send, z_recv, d_send, d_recv, local,
):
    me, mine = lax.axis_index("dp"), lax.axis_index("fsdp")
    greet(n_dp, n_f)
    orders = bit_orders(n_dp)
    for half in range(halves):
        for mask in sorted(range(n_dp), key=lambda m: 0 if m & 1 else 1):
            where = flip(me, mask)
            pltpu.make_async_copy(
                source.at[:, where, half], grads.at[:, where, half], load_sem.at[half, mask]
            ).start()
    started = exchange_start(n_dp, events, got_events, ev_send, ev_recv, local.at[0])
    z_copies = []

    def lane(half):
        order = orders[half % 2]
        yield from halving(
            order, n_dp, half, grads, out_buf, in_buf, h_send, h_recv, load_sem
        )
        for k in range(1, n_f):
            to = lax.rem(mine + k, n_f)
            z_out[half, k] = grads[to, me, half].astype(jnp.bfloat16)
            copy = pltpu.make_async_remote_copy(
                src_ref=z_out.at[half, k],
                dst_ref=z_in.at[half, k],
                send_sem=z_send.at[half, k],
                recv_sem=z_recv.at[half, k],
                device_id={"fsdp": to},
                device_id_type=MESH,
            )
            copy.start()
            z_copies.append(copy)
        yield True

        def ready():
            total = grads[mine, me, half]
            for k in range(1, n_f):
                wait_for(z_in.at[half, k], z_recv.at[half, k])
                total = total + z_in[half, k].astype(jnp.float32)
            summed[me, half] = total.astype(jnp.bfloat16)

        def buf(d):
            return summed.at[d, half]

        yield from doubling(order, n_dp, half, buf, d_send, d_recv, ready)

    for _ in staggered([lane(half) for half in range(halves)]):
        pass
    for copy in z_copies:
        copy.wait_send()
    exchange_finish(n_dp, started, got_events, ev_recv)


def reduce_grads(n_dp, n_f, grads, events):
    halves, rows, width = grads.shape[-3:]
    low = jnp.bfloat16
    return pl.pallas_call(
        functools.partial(reduce_kernel, n_dp, n_f, halves),
        out_shape=(
            jax.ShapeDtypeStruct(grads.shape[1:], low),
            jax.ShapeDtypeStruct(events.shape, low),
        ),
        in_specs=[pl.BlockSpec(memory_space=pl.ANY)] * 2,
        out_specs=[pl.BlockSpec(memory_space=pltpu.VMEM), pl.BlockSpec(memory_space=pl.ANY)],
        scratch_shapes=[
            pltpu.VMEM(grads.shape, jnp.float32),
            pltpu.VMEM((halves, n_dp - 1, n_f, rows, width), low),
            pltpu.VMEM((halves, n_dp - 1, n_f, rows, width), low),
            pltpu.VMEM((halves, n_f, rows, width), low),
            pltpu.VMEM((halves, n_f, rows, width), low),
            pltpu.SemaphoreType.DMA((halves, n_dp)),
            pltpu.SemaphoreType.DMA((n_dp,)),
            pltpu.SemaphoreType.DMA((n_dp,)),
            pltpu.SemaphoreType.DMA((halves, n_dp)),
            pltpu.SemaphoreType.DMA((halves, n_dp)),
            pltpu.SemaphoreType.DMA((halves, n_f)),
            pltpu.SemaphoreType.DMA((halves, n_f)),
            pltpu.SemaphoreType.DMA((halves, n_dp)),
            pltpu.SemaphoreType.DMA((halves, n_dp)),
            pltpu.SemaphoreType.DMA((1,)),
        ],
        compiler_params=pltpu.CompilerParams(
            collective_id=1, has_side_effects=True, vmem_limit_bytes=60 * MIB
        ),
    )(grads, events)


eps = 1e-05


def rms_scale(rows):
    return lax.rsqrt(jnp.mean(rows * rows, axis=-1, keepdims=True) + eps)


def rms_back(rows, factor, grad_out):
    cubed = factor * factor * factor
    return factor * grad_out - rows * cubed * jnp.mean(grad_out * rows, axis=-1, keepdims=True)


def dot_nn(left, right):
    return lax.dot_general(left, right, (((1,), (0,)), ((), ())), preferred_element_type=jnp.float32)


def dot_nt(left, right):
    return lax.dot_general(left, right, (((1,), (1,)), ((), ())), preferred_element_type=jnp.float32)


def dot_tn(left, right):
    return lax.dot_general(left, right, (((0,), (0,)), ((), ())), preferred_element_type=jnp.float32)


def window_kernel(
    grid, sizes, ids, attn, read, latents, unit_table, session_table, target, grads, grad_tokens,
    got_ids, full, id_send, id_recv, z_send, send, recv, local,
    tokens, normed, keys, values, query, mixed, gmixed, gquery, gkeys, gvalues, lat, lnorm, peak, scale,
    resid, ring, sems,
):
    n_dp, n_f, halves, lane_rows, slot_count = grid
    n_f, own, read_rows, lat_rows, out_width = sizes
    mine = lax.axis_index("fsdp")
    width = tokens.shape[1]
    low = jnp.bfloat16
    base_read = 4 * own
    base_lat = base_read + read_rows
    end = base_lat + lat_rows
    times = width // out_width
    W_Q, W_K, W_V, W_O = range(4)
    padded = full.shape[1]
    place = (padded - 2 * own, 0, own, padded - own)
    at_lat = 2 * own
    at_read = at_lat + lat_rows
    filled = at_read + read_rows

    moves = [(attn.at[k], full.at[mine, pl.ds(place[k], own)]) for k in range(4)]
    moves.append((latents, full.at[mine, pl.ds(at_lat, lat_rows)]))
    for t in range(times):
        moves.append((
            read.at[pl.ds(t * read_rows, read_rows)],
            full.at[mine, pl.ds(at_read, read_rows), pl.ds(t * out_width, out_width)],
        ))
    moves = [pltpu.make_async_copy(src, dst, local.at[1 + n]) for n, (src, dst) in enumerate(moves)]
    for move in moves:
        move.start()
    if filled < place[W_Q]:
        full[mine, filled:place[W_Q]] = jnp.zeros((place[W_Q] - filled, width), low)
    greet(n_dp, n_f)
    started = exchange_start(n_dp, ids, got_ids, id_send, id_recv, local.at[0])
    for move in moves:
        move.wait()
    progress, need, end_gather = gather(n_dp, n_f, halves, lane_rows, full, z_send, send, recv)
    exchange_finish(n_dp, started, got_ids, id_recv)
    state = {"n": 0, "busy": [None] * ring.shape[0]}

    def put(f, row, value):
        slot = state["n"] % ring.shape[0]
        state["n"] += 1
        if state["busy"][slot] is not None:
            state["busy"][slot].wait()
        rows = value.shape[0]
        ring[slot, pl.ds(0, rows)] = value
        copy = pltpu.make_async_copy(
            ring.at[slot, pl.ds(0, rows)], grads.at[f, pl.ds(row, rows)], sems.at[slot]
        )
        copy.start()
        state["busy"][slot] = copy

    def cols(f):
        return slice(f * own, (f + 1) * own)

    def block(k, f):
        return full[f, place[k]:place[k] + own]

    def times_weight(left, k):
        total = dot_nn(left[:, cols(0)], block(k, 0))
        for f in range(1, n_f):
            total = total + dot_nn(left[:, cols(f)], block(k, f))
        return total

    def grad_matrix(left, right, k):
        for f in range(n_f):
            put(f, k * own, dot_tn(left[:, cols(f)], right[...]))

    def slots(k):
        return jnp.concatenate(
            [got_ids[d, :, k * slot_count:(k + 1) * slot_count] for d in range(n_dp)], axis=1
        )

    slots_unit, slots_session, live = slots(0), slots(1), slots(2) > 0
    events = tokens.shape[0]

    def pick(table, ids, start, count):
        at = lax.broadcasted_iota(jnp.int32, (count, events), 0) + start
        return dot_tn((at == ids).astype(low), table[start:start + count])

    unit_rows = unit_table.shape[0]
    step = min(512, unit_rows)
    total = pick(unit_table, slots_unit, 0, step)
    for start in range(step, unit_rows, step):
        total = total + pick(unit_table, slots_unit, start, min(step, unit_rows - start))
    total = total + pick(session_table, slots_session, 0, session_table.shape[0])
    tokens[...] = total.astype(low)
    rows = tokens[...].astype(jnp.float32)
    normed[...] = (rows * rms_scale(rows)).astype(low)
    need(own)
    keys[...] = times_weight(normed, W_K).astype(low)
    need(2 * own)
    values[...] = times_weight(normed, W_V).astype(low)
    need(place[W_Q] + own)
    for f in range(n_f):
        lat[f * lat_rows:(f + 1) * lat_rows] = full[f, at_lat:at_lat + lat_rows]
    query[...] = times_weight(lat, W_Q).astype(low)

    latent_count = lat.shape[0]
    head_dim = width // HEADS
    head_factor = head_dim ** (-0.5)
    pack = 128 // head_dim
    which = lax.broadcasted_iota(jnp.int32, (1, 128), 1) // head_dim

    def masked(rows, part):
        return jnp.where(which == part, rows, jnp.zeros_like(rows))

    def merge(parts):
        out = parts[0]
        for part in range(1, pack):
            out = jnp.where(which == part, parts[part], out)
        return out

    def lanes(p):
        return pl.ds(pl.multiple_of(p * 128, 128), 128)

    def scores_of(q, k, part):
        return jnp.where(live, dot_nt(masked(q, part), k) * head_factor, -1e30)

    def forward(p, carry):
        q, k, v = query[:, lanes(p)], keys[:, lanes(p)], values[:, lanes(p)]
        outs = []
        for part in range(pack):
            s = scores_of(q, k, part)
            top = jnp.max(s, axis=-1, keepdims=True)
            w = jnp.where(live, jnp.exp(s - top), 0.0)
            inverse = 1.0 / jnp.sum(w, axis=-1, keepdims=True)
            peak[p * pack + part] = top
            scale[p * pack + part] = inverse
            outs.append(dot_nn((w * inverse).astype(low), v))
        mixed[:, lanes(p)] = merge(outs).astype(low)
        return carry

    lax.fori_loop(0, width // 128, forward, 0)

    end_gather()
    resid[...] = lat[...].astype(jnp.float32) + times_weight(mixed, W_O)
    factor = rms_scale(resid[...])
    lnorm[...] = (resid[...] * factor).astype(low)

    def pieces():
        step = own // times
        for f in range(n_f):
            for t in range(times):
                at = f * own + t * step
                yield f, t, slice(at, at + step), full[f, at_read:filled, t * out_width:(t + 1) * out_width]

    logits = None
    for f, t, at, weight in pieces():
        term = dot_nn(lnorm[:, at], weight)
        logits = term if logits is None else logits + term
    glogits = (
        (jax.nn.sigmoid(logits) - target[...].astype(jnp.float32)) * latent_count ** (-0.5)
    ).astype(low)
    for f in range(n_f):
        put(f, base_read, jnp.concatenate(
            [dot_tn(lnorm[:, at], glogits) for g, t, at, _ in pieces() if g == f], axis=1
        ))
    glnorm = jnp.concatenate([dot_nt(glogits, weight) for _, _, _, weight in pieces()], axis=1)
    gresid = rms_back(resid[...], factor, glnorm)
    resid[...] = gresid
    gresid_low = gresid.astype(low)
    for f in range(n_f):
        gmixed[:, cols(f)] = dot_nt(gresid_low, block(W_O, f)).astype(low)
    lnorm[...] = gresid_low
    grad_matrix(mixed, lnorm, W_O)

    def backward(p, carry):
        q, k, v, g = query[:, lanes(p)], keys[:, lanes(p)], values[:, lanes(p)], gmixed[:, lanes(p)]
        outs = ([], [], [])
        for part in range(pack):
            s = scores_of(q, k, part)
            probs = jnp.where(live, jnp.exp(s - peak[p * pack + part]), 0.0) * scale[p * pack + part]
            gprobs = dot_nt(masked(g, part), v)
            inner = jnp.sum(gprobs * probs, axis=-1, keepdims=True)
            gscores = (probs * (gprobs - inner) * head_factor).astype(low)
            outs[0].append(dot_tn(probs.astype(low), g))
            outs[1].append(dot_nn(gscores, k))
            outs[2].append(dot_tn(gscores, q))
        gvalues[:, lanes(p)] = merge(outs[0]).astype(low)
        gquery[:, lanes(p)] = merge(outs[1]).astype(low)
        gkeys[:, lanes(p)] = merge(outs[2]).astype(low)
        return carry

    lax.fori_loop(0, width // 128, backward, 0)

    grad_matrix(lat, gquery, W_Q)
    for f in range(n_f):
        resid[:, cols(f)] += dot_nt(gquery[...], block(W_Q, f))
    for f in range(n_f):
        put(f, base_lat, resid[f * lat_rows:(f + 1) * lat_rows])
    grad_matrix(normed, gkeys, W_K)
    grad_matrix(normed, gvalues, W_V)
    spare = grads.shape[1] - end
    if spare:
        for f in range(n_f):
            put(f, end, jnp.zeros((spare, width), jnp.float32))
    gnormed = jnp.concatenate(
        [
            dot_nt(gkeys[...], block(W_K, f)) + dot_nt(gvalues[...], block(W_V, f))
            for f in range(n_f)
        ],
        axis=1,
    )
    rows = tokens[...].astype(jnp.float32)
    grad_tokens[...] = rms_back(rows, rms_scale(rows), gnormed).astype(low)
    for copy in state["busy"]:
        if copy is not None:
            copy.wait()


def window_grads(grid, sizes, ids, attn, read, latents, unit_table, session_table, target):
    n_dp, n_f, halves, lane_rows, slot_count = grid
    n_f, own, read_rows, lat_rows, out_width = sizes
    events, width = n_dp * slot_count, attn.shape[-1]
    latent_count = n_f * lat_rows
    low = jnp.bfloat16
    padded = halves * n_dp * lane_rows
    ring_rows = max(own, padded - 4 * own - read_rows - lat_rows)
    by_event = pltpu.VMEM((events, width), low)
    by_latent = pltpu.VMEM((latent_count, width), low)
    column = pltpu.VMEM((HEADS, latent_count, 1), jnp.float32)
    in_vmem, anywhere = pl.BlockSpec(memory_space=pltpu.VMEM), pl.BlockSpec(memory_space=pl.ANY)
    return pl.pallas_call(
        functools.partial(window_kernel, grid, sizes),
        out_shape=(
            jax.ShapeDtypeStruct((n_f, padded, width), jnp.float32),
            jax.ShapeDtypeStruct((events, width), low),
        ),
        in_specs=[in_vmem] + [anywhere] * 3 + [in_vmem] * 3,
        out_specs=[anywhere, in_vmem],
        scratch_shapes=[
            pltpu.VMEM(ids.shape, ids.dtype),
            pltpu.VMEM((n_f, padded, width), low),
            pltpu.SemaphoreType.DMA((n_dp,)),
            pltpu.SemaphoreType.DMA((n_dp,)),
            pltpu.SemaphoreType.DMA((halves, n_f)),
            pltpu.SemaphoreType.DMA((n_f, halves, n_dp)),
            pltpu.SemaphoreType.DMA((n_f, halves, n_dp)),
            pltpu.SemaphoreType.DMA((6 + width // out_width,)),
            by_event, by_event, by_event, by_event,
            by_latent, by_latent, by_latent, by_latent,
            by_event, by_event, by_latent, by_latent, column, column,
            pltpu.VMEM((latent_count, width), jnp.float32),
            pltpu.VMEM((4, ring_rows, width), jnp.float32),
            pltpu.SemaphoreType.DMA((4,)),
        ],
        compiler_params=pltpu.CompilerParams(
            collective_id=0, has_side_effects=True, vmem_limit_bytes=60 * MIB
        ),
    )(ids, attn, read, latents, unit_table, session_table, target)


def piece_rows(rows, n_dp):
    options = []
    for lanes in range(1, 6):
        lane_rows = -(-rows // (n_dp * lanes * 16)) * 16
        options.append((lane_rows * lanes, -lanes, lane_rows))
    _, lanes, lane_rows = min(options)
    return lane_rows, -lanes


def unfold(rows, narrow):
    times = rows.shape[-1] // narrow
    return jnp.concatenate(
        [rows[..., k * narrow:(k + 1) * narrow] for k in range(times)], axis=-2
    )


def on_device(
    unit_ids,
    session_ids,
    counts,
    targets,
    unit_table,
    session_table,
    attn_weights,
    read_weight,
    latents,
):
    n_dp, n_f = lax.axis_size("dp"), lax.axis_size("fsdp")
    slot_count = unit_ids.shape[-1]
    width = unit_table.shape[1]
    event_total = n_dp * slot_count
    stack, own_rows, _ = attn_weights.shape
    read_rows = read_weight.size // width
    lat_rows = latents.shape[0]
    out_width = read_weight.shape[1]
    ends = (stack * own_rows, stack * own_rows + read_rows, stack * own_rows + read_rows + lat_rows)
    rows, halves = piece_rows(ends[2], n_dp)
    padded = rows * halves * n_dp

    id_rows = jnp.concatenate(
        [
            unit_ids.reshape(n_dp, slot_count),
            session_ids.reshape(n_dp, slot_count),
            (jnp.arange(slot_count, dtype=jnp.int32) < counts.reshape(n_dp, 1)).astype(jnp.int32),
        ],
        axis=1,
    )
    id_rows = jnp.pad(id_rows, ((0, 0), (0, 128 - id_rows.shape[1]))).reshape(n_dp, 1, 128)
    grads, grad_tokens = window_grads(
        (n_dp, n_f, halves, rows, slot_count),
        (n_f, own_rows, read_rows, lat_rows, out_width),
        id_rows,
        attn_weights,
        read_weight,
        latents,
        unit_table,
        session_table,
        targets.reshape(targets.shape[-2], out_width),
    )
    grads = grads.reshape(n_f, n_dp, halves, rows, width)
    summed, event_grad = reduce_grads(
        n_dp, n_f, grads, grad_tokens.reshape(n_dp, slot_count, width)
    )
    summed = summed.reshape(padded, width)
    return (
        event_grad.reshape(unit_ids.shape + (width,)),
        summed[:ends[0]].reshape(stack, own_rows, width).astype(jnp.float32),
        unfold(summed[ends[0]:ends[1]], out_width).astype(jnp.float32),
        summed[ends[1]:ends[2]].astype(jnp.float32),
    )


def solution(mesh):
    placed = (
        P("fsdp", "dp", None, None),
        P("fsdp", "dp", None, None),
        P("fsdp", "dp", None),
        P("fsdp", "dp", None, None),
        P(),
        P(),
        P(None, "fsdp", None),
        P("fsdp", None),
        P("fsdp", None),
    )
    return jax.shard_map(
        on_device,
        mesh=mesh,
        in_specs=placed,
        out_specs=(
            P("fsdp", "dp", None, None, None),
            P(None, "fsdp", None),
            P("fsdp", None),
            P("fsdp", None),
        ),
        check_vma=False,
    )
```
